32 devices in a mesh: blk: 16 (over z, y, core), lag: 2 (over x).
Axes of the slice: x: 2, y: 2, z: 4, core: 2. Of those that a mesh axis runs over, the one named last changes fastest.
Arguments:
- spectra: bfloat16 [2048, 3, 2, 1024], P('blk', None, None, 'lag'), may hold values from -6 to 6
- band: int32 [2048, 2], P('blk'), may hold values from 0 to 1024, as said below
- pair_lists: int32 [16, 9, 96, 2], P('blk'), may hold values from 0 to 127
- pair_counts: int32 [16, 9], P('blk'), may hold values from 32 to 96, as said below
Outputs:
- gradient: float32 [2048, 3, 2, 1024], P('blk', None, None, 'lag')
The draws below stay inside these ranges and needn't reach their ends.
Inputs may be any that keep to these rules, and one draw needn't show every extreme that they name: band[s, 0] < band[s, 1]; band[s, 0] is at most 128 and band[s, 1] at least 896; some station starts at 0 and some ends at 1024. `pair_counts`: at least a third of the slots are used; in every block one offset uses all 96 slots.
All inputs are finite; a program needn't handle non-finite values.
Results may differ from the reference program's by a relative error of at most 0.0045.
Values may be sent and summed in bfloat16 or wider, within the bound.
A program may use at most 64 MiB of HBM per device.

```python
import jax
import jax.numpy as jnp
from jax import lax

STA_DEV = 128
P_MAX = 96
F = 1024
LAGS = 2048
BLOCKS = 16
STEPS = 9
STATIONS = 2048


def draw_spectra(key, part):
    base = jax.random.fold_in(key, 37)
    key_noise, key_common, key_sign = jax.random.split(base, 3)
    shape = (STATIONS, 3, 2, F)
    signs = (jax.random.randint(key_sign, (STATIONS, 1, 1, 1), 0, 2) * 2 - 1).astype(jnp.float32)
    noise = jax.random.normal(key_noise, shape, jnp.float32)
    common = jnp.clip(jax.random.normal(key_common, (1, 3, 2, F), jnp.float32), -2.5, 2.5)
    amplitude = jnp.ones((F,), jnp.float32)
    values = noise + signs * amplitude[None, None, None, :] * common
    return jnp.clip(values, -6.0, 6.0).astype(jnp.bfloat16)


def draw_band(key, part):
    key_lo, key_hi, key_first, key_last = jax.random.split(jax.random.fold_in(key, 11), 4)
    lower = jax.random.randint(key_lo, (STATIONS,), 0, F // 8 + 1)
    upper = jax.random.randint(key_hi, (STATIONS,), F - F // 8, F + 1)
    station_ids = jnp.arange(STATIONS, dtype=jnp.int32)
    first_pick = jax.random.randint(key_first, (), 0, STATIONS)
    last_pick = jax.random.randint(key_last, (), 0, STATIONS)
    lower = jnp.where(station_ids == first_pick, 0, lower)
    upper = jnp.where(station_ids == last_pick, F, upper)
    return jnp.stack([lower, upper], 1).astype(jnp.int32)


def draw_pair_counts(key, part):
    key_base, key_full = jax.random.split(jax.random.fold_in(key, 23))
    base = jax.random.randint(key_base, (BLOCKS, STEPS), P_MAX // 3, P_MAX + 1)
    full_step = jax.random.randint(key_full, (BLOCKS, 1), 0, STEPS)
    step_ids = jnp.arange(STEPS, dtype=jnp.int32)[None, :]
    return jnp.where(step_ids == full_step, P_MAX, base).astype(jnp.int32)


def with_ends(entries, rng, smallest, top_value):
    longest = entries.shape.index(max(entries.shape))
    spots = []
    for shift in (0, 1):
        where = [jax.random.randint(jax.random.fold_in(rng, axis), (), 0, length) for axis, length in enumerate(entries.shape)]
        where[longest] = (where[longest] + shift) % entries.shape[longest]
        spots.append(tuple(where))
    return entries.at[spots[0]].set(smallest).at[spots[1]].set(top_value)


def setup_inputs(seed: int = 0) -> dict:
    keys = jax.random.split(jax.random.key(seed), 5)
    return {
        "spectra": draw_spectra(jax.random.fold_in(keys[4], 71), 0),
        "band": draw_band(jax.random.fold_in(keys[4], 71), 0),
        "pair_lists": with_ends(jax.random.randint(keys[2], (BLOCKS, STEPS, P_MAX, 2), 0, STA_DEV), jax.random.fold_in(keys[2], 1), 0, STA_DEV - 1).astype(jnp.int32),
        "pair_counts": draw_pair_counts(jax.random.fold_in(keys[4], 71), 0),
    }


def phase_table(freq_ids, lag_ids, lag_total, freq_total):
    turns = freq_ids[:, None] * lag_ids[None, :] % lag_total
    angle = turns.astype(jnp.float32) * (2.0 * jnp.pi / lag_total)
    factor = 1.0 / jnp.sqrt(jnp.float32(freq_total))
    return jnp.stack([jnp.cos(angle) * factor, -jnp.sin(angle) * factor], 0).astype(jnp.bfloat16)

def whiten(spectra, band, freq_ids):
    values = spectra.astype(jnp.float32)
    meansq = lax.optimization_barrier(jnp.mean(values * values, axis=(1, 2)))
    inside = (freq_ids[None, :] >= band[:, 0:1]) & (freq_ids[None, :] < band[:, 1:2])
    factor = jnp.where(inside, 1.0 / jnp.sqrt(jnp.maximum(meansq, 0.25)), 0.0)
    return (values * factor[:, None, None, :]).astype(jnp.bfloat16)

def reference(spectra, band, pair_lists, pair_counts):
    freq_ids = jnp.arange(F, dtype=jnp.int32)
    whitened = whiten(spectra, band, freq_ids)
    table = phase_table(freq_ids, jnp.arange(LAGS, dtype=jnp.int32), LAGS, F)
    table_flat = table.reshape(2 * F, LAGS).astype(jnp.float32)
    weight = 1.0 + 3.0 * jnp.arange(LAGS, dtype=jnp.int32).astype(jnp.float32) / LAGS
    blocked = whitened.reshape(BLOCKS, STA_DEV, 3, 2, F)
    offsets = jnp.arange(STEPS, dtype=jnp.int32)
    slot_ids = jnp.arange(P_MAX, dtype=jnp.int32)

    def per_block(block, grad):
        block = block.astype(jnp.int32)
        pairs = pair_lists[block]
        counts = pair_counts[block]
        others = (block - offsets) % BLOCKS
        first = pairs[:, :, 0]
        second = pairs[:, :, 1]
        rows_a = blocked[block][first].astype(jnp.float32)
        rows_b = blocked[others[:, None], second].astype(jnp.float32)
        real_a, imag_a = (rows_a[:, :, :, 0], rows_a[:, :, :, 1])
        real_b, imag_b = (rows_b[:, :, :, 0], rows_b[:, :, :, 1])
        valid = (slot_ids[None, :] < counts[:, None]).astype(jnp.float32)[:, :, None]
        cross_real = lax.optimization_barrier(jnp.sum(real_a * real_b + imag_a * imag_b, axis=2)) * valid
        cross_imag = lax.optimization_barrier(jnp.sum(imag_a * real_b - real_a * imag_b, axis=2)) * valid
        cross = jnp.stack([cross_real, cross_imag], 2).astype(jnp.bfloat16)
        cross_flat = cross.reshape(STEPS * P_MAX, 2 * F).astype(jnp.float32)
        lagged = jnp.dot(cross_flat, table_flat, precision=lax.Precision.HIGHEST)
        energy = lax.optimization_barrier(jnp.sum(weight[None, :] * lagged * lagged, axis=1)) / LAGS
        adjoint = (weight[None, :] * lagged / jnp.sqrt(energy + 1e-05)[:, None]).astype(jnp.bfloat16)
        spectral = jnp.dot(adjoint.astype(jnp.float32), table_flat.T, precision=lax.Precision.HIGHEST)
        spectral = spectral.reshape(STEPS, P_MAX, 2, F)
        adj_real = spectral[:, :, None, 0]
        adj_imag = spectral[:, :, None, 1]
        near = jnp.stack([adj_real * real_b - adj_imag * imag_b, adj_real * imag_b + adj_imag * real_b], 3).astype(jnp.bfloat16)
        far = jnp.stack([adj_real * real_a + adj_imag * imag_a, adj_real * imag_a - adj_imag * real_a], 3).astype(jnp.bfloat16)
        grad = grad.at[block * STA_DEV + first].add(near.astype(jnp.float32))
        grad = grad.at[others[:, None] * STA_DEV + second].add(far.astype(jnp.float32))
        return grad
    grad = lax.fori_loop(0, BLOCKS, per_block, jnp.zeros((STATIONS, 3, 2, F), jnp.float32))
    return grad / jnp.sqrt(jnp.float32(P_MAX))
```

```python
import math

import jax
import jax.numpy as jnp
import ml_dtypes
import numpy as np
from jax import lax
from jax.sharding import PartitionSpec as P

F32 = jnp.float32
BF16 = jnp.bfloat16


def from_behind(block, axis, distance):
    devices = range(lax.axis_size(axis))
    route = [((i - distance) % len(devices), i) for i in devices]
    return lax.ppermute(block, axis, route)


def phase_table(lanes, bins_local):
    freq_total = lanes * bins_local
    lag_total = 2 * freq_total
    turns = np.arange(freq_total)[:, None] * np.arange(lag_total)[None, :] % lag_total
    angle = turns.astype(np.float32) * np.float32(2.0 * np.pi / lag_total)
    factor = np.float32(1.0) / np.sqrt(np.float32(freq_total))
    table = np.stack([np.cos(angle) * factor, -np.sin(angle) * factor], 0)
    table = table.reshape(2, lanes, bins_local, lag_total).transpose(1, 0, 2, 3)
    return table.reshape(lanes * 2 * bins_local, lag_total).astype(ml_dtypes.bfloat16)


def whiten(spectra, band, freq_ids):
    values = spectra.astype(F32)
    meansq = jnp.mean(values * values, axis=(1, 2))
    inside = (freq_ids[None, :] >= band[:, 0:1]) & (freq_ids[None, :] < band[:, 1:2])
    factor = jnp.where(inside, 1.0 / jnp.sqrt(jnp.maximum(meansq, 0.25)), 0.0)
    return (values * factor[:, None, None, :]).astype(BF16)


def in_lane_order(own, received, lane, lanes):
    relative = [own] + received
    backward = [relative[(-m) % lanes] for m in range(lanes)]
    if lanes == 2:
        first = jnp.where(lane == 0, own, received[0])
        second = jnp.where(lane == 0, received[0], own)
        return [first, second]
    stacked = jnp.stack(backward + backward, 0)
    ordered = lax.dynamic_slice_in_dim(stacked, (lanes - lane) % lanes, lanes, 0)
    return [ordered[j] for j in range(lanes)]


def swap_lanes(pieces, lane, lanes):
    stacked = jnp.stack(pieces, 0)
    own = lax.dynamic_index_in_dim(stacked, lane, 0, keepdims=False)
    received = []
    for r in range(1, lanes):
        leaving = lax.dynamic_index_in_dim(stacked, (lane + r) % lanes, 0, keepdims=False)
        received.append(from_behind(leaving, "lag", r))
    return in_lane_order(own, received, lane, lanes)


def on_device(spectra, band, pair_lists, pair_counts):
    stations, comps, parts, bins = spectra.shape
    steps, slots = pair_lists.shape[1:3]
    lanes = lax.axis_size("lag")
    freq_total = bins * lanes
    lag_total = 2 * freq_total
    width = comps * parts * bins
    lane = lax.axis_index("lag")
    freq_ids = lane * bins + jnp.arange(bins, dtype=jnp.int32)
    reach = math.isqrt(steps - 1) + 1
    aheads = list(range(reach))
    behinds = list(range(0, steps, reach))

    slot_ids = jnp.arange(slots, dtype=jnp.int32)
    used = slot_ids[None, :] < pair_counts[0][:, None]
    lists = jnp.where(used[:, :, None], pair_lists[0], stations)
    lists_of = {0: lists}
    for ahead in aheads[1:]:
        lists_of[ahead] = from_behind(lists, "blk", -ahead)
    resident = whiten(spectra, band, freq_ids).reshape(stations, width)
    firsts = {0: resident}
    seconds = {0: resident}
    for ahead in aheads[1:]:
        firsts[ahead] = from_behind(resident, "blk", -ahead)
    order = [0] + behinds[:0:-1]
    for behind in order[1:]:
        seconds[behind] = from_behind(resident, "blk", behind)

    table = jnp.asarray(phase_table(lanes, bins))
    weight = 1.0 + 3.0 * jnp.arange(lag_total, dtype=F32) / lag_total
    station_ids = jnp.arange(stations, dtype=jnp.int32)

    def planes(rows):
        return [rows[:, i * bins : (i + 1) * bins].astype(F32) for i in range(comps * parts)]

    total_first = {ahead: [] for ahead in aheads}
    returned = []
    for behind in order:
        active = [ahead for ahead in aheads if ahead + behind < steps]
        chosen = jnp.concatenate([lists_of[a][a + behind] for a in active], 0)
        pick_first = (chosen[:, 0:1] == station_ids[None, :]).astype(BF16)
        pick_second = (chosen[:, 1:2] == station_ids[None, :]).astype(BF16)
        rows_a = jnp.concatenate(
            [
                jnp.dot(pick_first[n * slots : (n + 1) * slots], firsts[a], preferred_element_type=BF16)
                for n, a in enumerate(active)
            ],
            0,
        )
        rows_b = jnp.dot(pick_second, seconds[behind], preferred_element_type=BF16)
        a = planes(rows_a)
        b = planes(rows_b)
        real = sum(a[2 * c] * b[2 * c] + a[2 * c + 1] * b[2 * c + 1] for c in range(comps))
        imag = sum(a[2 * c + 1] * b[2 * c] - a[2 * c] * b[2 * c + 1] for c in range(comps))
        cross = jnp.concatenate([real, imag], 1).astype(BF16)
        share = cross.shape[0] // lanes
        full = jnp.concatenate(
            swap_lanes([cross[j * share : (j + 1) * share] for j in range(lanes)], lane, lanes), 1
        )
        lagged = jnp.dot(full, table, preferred_element_type=F32)
        energy = jnp.sum(weight[None, :] * lagged * lagged, axis=1) / lag_total
        adjoint = (weight[None, :] * lagged / jnp.sqrt(energy + 1e-05)[:, None]).astype(BF16)
        spectral = lax.dot_general(
            adjoint, table, (((1,), (1,)), ((), ())), preferred_element_type=F32
        ).astype(BF16)
        mine = 2 * bins
        spectral = jnp.concatenate(
            swap_lanes([spectral[:, j * mine : (j + 1) * mine] for j in range(lanes)], lane, lanes), 0
        ).astype(F32)
        real = spectral[:, :bins]
        imag = spectral[:, bins:]
        near = []
        far = []
        for c in range(comps):
            near += [real * b[2 * c] - imag * b[2 * c + 1], real * b[2 * c + 1] + imag * b[2 * c]]
            far += [real * a[2 * c] + imag * a[2 * c + 1], real * a[2 * c + 1] - imag * a[2 * c]]
        near = jnp.concatenate(near, 1).astype(BF16)
        far = jnp.concatenate(far, 1).astype(BF16)
        for n, ahead in enumerate(active):
            total_first[ahead].append(
                (pick_first[n * slots : (n + 1) * slots], near[n * slots : (n + 1) * slots])
            )
        if behind == 0:
            total_first[0].append((pick_second, far))
        else:
            back = jnp.einsum("ps,pw->sw", pick_second, far, preferred_element_type=F32)
            returned.append(from_behind(back.astype(BF16), "blk", -behind))

    def scatter(terms):
        picks = jnp.concatenate([pick for pick, _ in terms], 0)
        values = jnp.concatenate([value for _, value in terms], 0)
        return jnp.einsum("ps,pw->sw", picks, values, preferred_element_type=F32)

    for ahead in aheads[:0:-1]:
        returned.append(from_behind(scatter(total_first[ahead]).astype(BF16), "blk", ahead))
    total = scatter(total_first[0])
    for part in returned:
        total = total + part.astype(F32)
    gradient = total / math.sqrt(slots)
    return gradient.reshape(stations, comps, parts, bins)


def solution(mesh):
    in_specs = (
        P("blk", None, None, "lag"),
        P("blk", None),
        P("blk", None, None, None),
        P("blk", None),
    )
    out_specs = P("blk", None, None, "lag")
    return jax.shard_map(
        on_device, mesh=mesh, in_specs=in_specs, out_specs=out_specs, check_vma=False
    )
```

```python
import math

import jax
import jax.numpy as jnp
import ml_dtypes
import numpy as np
from jax import lax
from jax.sharding import PartitionSpec as P

F32 = jnp.float32
BF16 = jnp.bfloat16


def from_behind(block, axis, distance):
    devices = range(lax.axis_size(axis))
    route = [((i - distance) % len(devices), i) for i in devices]
    return lax.ppermute(block, axis, route)


def phase_table(lanes, bins_local):
    freq_total = lanes * bins_local
    lag_total = 2 * freq_total
    turns = np.arange(freq_total)[:, None] * np.arange(lag_total)[None, :] % lag_total
    angle = turns.astype(np.float32) * np.float32(2.0 * np.pi / lag_total)
    factor = np.float32(1.0) / np.sqrt(np.float32(freq_total))
    table = np.stack([np.cos(angle) * factor, -np.sin(angle) * factor], 0)
    table = table.reshape(2, lanes, bins_local, lag_total).transpose(1, 0, 2, 3)
    return table.reshape(lanes * 2 * bins_local, lag_total).astype(ml_dtypes.bfloat16)


def whiten(spectra, band, freq_ids):
    values = spectra.astype(F32)
    meansq = jnp.mean(values * values, axis=(1, 2))
    inside = (freq_ids[None, :] >= band[:, 0:1]) & (freq_ids[None, :] < band[:, 1:2])
    factor = jnp.where(inside, 1.0 / jnp.sqrt(jnp.maximum(meansq, 0.25)), 0.0)
    return (values * factor[:, None, None, :]).astype(BF16)


def in_lane_order(own, received, lane, lanes):
    relative = [own] + received
    backward = [relative[(-m) % lanes] for m in range(lanes)]
    if lanes == 2:
        first = jnp.where(lane == 0, own, received[0])
        second = jnp.where(lane == 0, received[0], own)
        return [first, second]
    stacked = jnp.stack(backward + backward, 0)
    ordered = lax.dynamic_slice_in_dim(stacked, (lanes - lane) % lanes, lanes, 0)
    return [ordered[j] for j in range(lanes)]


def swap_lanes(pieces, lane, lanes):
    stacked = jnp.stack(pieces, 0)
    own = lax.dynamic_index_in_dim(stacked, lane, 0, keepdims=False)
    received = []
    for r in range(1, lanes):
        leaving = lax.dynamic_index_in_dim(stacked, (lane + r) % lanes, 0, keepdims=False)
        received.append(from_behind(leaving, "lag", r))
    return in_lane_order(own, received, lane, lanes)


def on_device(spectra, band, pair_lists, pair_counts):
    stations, comps, parts, bins = spectra.shape
    steps, slots = pair_lists.shape[1:3]
    lanes = lax.axis_size("lag")
    freq_total = bins * lanes
    lag_total = 2 * freq_total
    width = comps * parts * bins
    lane = lax.axis_index("lag")
    freq_ids = lane * bins + jnp.arange(bins, dtype=jnp.int32)
    reach = math.isqrt(steps - 1) + 1
    aheads = list(range(reach))
    behinds = list(range(0, steps, reach))

    slot_ids = jnp.arange(slots, dtype=jnp.int32)
    used = slot_ids[None, :] < pair_counts[0][:, None]
    lists = jnp.where(used[:, :, None], pair_lists[0], stations)
    lists_of = {0: lists}
    for ahead in aheads[1:]:
        lists_of[ahead] = from_behind(lists, "blk", -ahead)
    resident = whiten(spectra, band, freq_ids).reshape(stations, width)
    firsts = {0: resident}
    seconds = {0: resident}
    for behind in behinds[1:]:
        seconds[behind] = from_behind(seconds[behind - reach], "blk", reach)
    for ahead in aheads[1:]:
        firsts[ahead] = from_behind(firsts[ahead - 1], "blk", -1)

    table = jnp.asarray(phase_table(lanes, bins))
    weight = 1.0 + 3.0 * jnp.arange(lag_total, dtype=F32) / lag_total
    station_ids = jnp.arange(stations, dtype=jnp.int32)

    def planes(rows):
        return [rows[:, i * bins : (i + 1) * bins].astype(F32) for i in range(comps * parts)]

    pairs_first = {ahead: [] for ahead in aheads}
    pairs_second = {behind: [] for behind in behinds}
    rounds = {}
    for ahead in aheads:
        for behind in behinds:
            if ahead + behind < steps:
                arrival = max(ahead, behind // reach, 1)
                rounds.setdefault(arrival, []).append((ahead, behind))
    after = jnp.int32(0)
    for arrival in sorted(rounds):
        active = rounds[arrival]
        picks = []
        rows = []
        crosses = []
        for ahead, behind in active:
            chosen = lists_of[ahead][ahead + behind] + after
            pick_first = (chosen[:, 0:1] == station_ids[None, :]).astype(BF16)
            pick_second = (chosen[:, 1:2] == station_ids[None, :]).astype(BF16)
            a = planes(jnp.dot(pick_first, firsts[ahead], preferred_element_type=BF16))
            b = planes(jnp.dot(pick_second, seconds[behind], preferred_element_type=BF16))
            real = sum(a[2 * c] * b[2 * c] + a[2 * c + 1] * b[2 * c + 1] for c in range(comps))
            imag = sum(a[2 * c + 1] * b[2 * c] - a[2 * c] * b[2 * c + 1] for c in range(comps))
            picks.append((pick_first, pick_second))
            rows.append((a, b))
            crosses.append(jnp.concatenate([real, imag], 1).astype(BF16))
        cross = jnp.concatenate(crosses, 0)
        share = cross.shape[0] // lanes
        full = jnp.concatenate(
            swap_lanes([cross[j * share : (j + 1) * share] for j in range(lanes)], lane, lanes), 1
        )
        lagged = jnp.dot(full, table, preferred_element_type=F32)
        energy = jnp.sum(weight[None, :] * lagged * lagged, axis=1) / lag_total
        adjoint = (weight[None, :] * lagged / jnp.sqrt(energy + 1e-05)[:, None]).astype(BF16)
        spectral = lax.dot_general(
            adjoint, table, (((1,), (1,)), ((), ())), preferred_element_type=F32
        ).astype(BF16)
        after = jnp.minimum(jnp.abs(spectral[0, 0]), 0).astype(jnp.int32)
        mine = 2 * bins
        spectral = jnp.concatenate(
            swap_lanes([spectral[:, j * mine : (j + 1) * mine] for j in range(lanes)], lane, lanes), 0
        )
        for n, (ahead, behind) in enumerate(active):
            a, b = rows[n]
            listed = spectral[n * slots : (n + 1) * slots].astype(F32)
            real = listed[:, :bins]
            imag = listed[:, bins:]
            near = []
            far = []
            for c in range(comps):
                near += [real * b[2 * c] - imag * b[2 * c + 1], real * b[2 * c + 1] + imag * b[2 * c]]
                far += [real * a[2 * c] + imag * a[2 * c + 1], real * a[2 * c + 1] - imag * a[2 * c]]
            near = jnp.concatenate(near, 1).astype(BF16)
            far = jnp.concatenate(far, 1).astype(BF16)
            pairs_first[ahead].append((picks[n][0], near))
            pairs_second[behind].append((picks[n][1], far))

    def scatter(terms):
        picks = jnp.concatenate([pick for pick, _ in terms], 0)
        values = jnp.concatenate([value for _, value in terms], 0)
        return jnp.einsum("ps,pw->sw", picks, values, preferred_element_type=F32)

    from_ahead = jnp.zeros((), F32)
    from_back = jnp.zeros((), F32)
    for behind in behinds[:0:-1]:
        part = scatter(pairs_second[behind]) + from_back
        from_back = from_behind(part.astype(BF16), "blk", -reach).astype(F32)
    for ahead in aheads[:0:-1]:
        part = scatter(pairs_first[ahead]) + from_ahead
        from_ahead = from_behind(part.astype(BF16), "blk", 1).astype(F32)
    total = scatter(pairs_first[0] + pairs_second[0]) + from_back + from_ahead
    gradient = total / math.sqrt(slots)
    return gradient.reshape(stations, comps, parts, bins)


def solution(mesh):
    in_specs = (
        P("blk", None, None, "lag"),
        P("blk", None),
        P("blk", None, None, None),
        P("blk", None),
    )
    out_specs = P("blk", None, None, "lag")
    return jax.shard_map(
        on_device, mesh=mesh, in_specs=in_specs, out_specs=out_specs, check_vma=False
    )
```

```python
import math

import jax
import jax.numpy as jnp
import ml_dtypes
import numpy as np
from jax import lax
from jax.sharding import PartitionSpec as P

F32 = jnp.float32
BF16 = jnp.bfloat16


def from_behind(block, axis, distance):
    devices = range(lax.axis_size(axis))
    route = [((i - distance) % len(devices), i) for i in devices]
    return lax.ppermute(block, axis, route)


def phase_table(lanes, bins_local):
    freq_total = lanes * bins_local
    lag_total = 2 * freq_total
    turns = np.arange(freq_total)[:, None] * np.arange(lag_total)[None, :] % lag_total
    angle = turns.astype(np.float32) * np.float32(2.0 * np.pi / lag_total)
    factor = np.float32(1.0) / np.sqrt(np.float32(freq_total))
    table = np.stack([np.cos(angle) * factor, -np.sin(angle) * factor], 0)
    table = table.reshape(2, lanes, bins_local, lag_total).transpose(1, 0, 2, 3)
    return table.reshape(lanes * 2 * bins_local, lag_total).astype(ml_dtypes.bfloat16)


def whiten(spectra, band, freq_ids):
    values = spectra.astype(F32)
    meansq = jnp.mean(values * values, axis=(1, 2))
    inside = (freq_ids[None, :] >= band[:, 0:1]) & (freq_ids[None, :] < band[:, 1:2])
    factor = jnp.where(inside, 1.0 / jnp.sqrt(jnp.maximum(meansq, 0.25)), 0.0)
    return (values * factor[:, None, None, :]).astype(BF16)


def in_lane_order(own, received, lane, lanes):
    relative = [own] + received
    backward = [relative[(-m) % lanes] for m in range(lanes)]
    if lanes == 2:
        first = jnp.where(lane == 0, own, received[0])
        second = jnp.where(lane == 0, received[0], own)
        return [first, second]
    stacked = jnp.stack(backward + backward, 0)
    ordered = lax.dynamic_slice_in_dim(stacked, (lanes - lane) % lanes, lanes, 0)
    return [ordered[j] for j in range(lanes)]


def swap_lanes(pieces, lane, lanes):
    stacked = jnp.stack(pieces, 0)
    own = lax.dynamic_index_in_dim(stacked, lane, 0, keepdims=False)
    received = []
    for r in range(1, lanes):
        leaving = lax.dynamic_index_in_dim(stacked, (lane + r) % lanes, 0, keepdims=False)
        received.append(from_behind(leaving, "lag", r))
    return in_lane_order(own, received, lane, lanes)


def on_device(spectra, band, pair_lists, pair_counts):
    stations, comps, parts, bins = spectra.shape
    steps, slots = pair_lists.shape[1:3]
    lanes = lax.axis_size("lag")
    freq_total = bins * lanes
    lag_total = 2 * freq_total
    width = comps * parts * bins
    lane = lax.axis_index("lag")
    freq_ids = lane * bins + jnp.arange(bins, dtype=jnp.int32)
    reach = math.isqrt(steps - 1) + 1
    aheads = list(range(reach))
    behinds = list(range(0, steps, reach))

    slot_ids = jnp.arange(slots, dtype=jnp.int32)
    used = slot_ids[None, :] < pair_counts[0][:, None]
    lists = jnp.where(used[:, :, None], pair_lists[0], stations)
    lists_of = {0: lists}
    for ahead in aheads[1:]:
        lists_of[ahead] = from_behind(lists, "blk", -ahead)
    resident = whiten(spectra, band, freq_ids).reshape(stations, width)
    firsts = {0: resident}
    seconds = {0: resident}
    for behind in behinds[1:]:
        seconds[behind] = from_behind(seconds[behind - reach], "blk", reach)
    for ahead in aheads[1:]:
        firsts[ahead] = from_behind(firsts[ahead - 1], "blk", -1)

    table = jnp.asarray(phase_table(lanes, bins))
    weight = 1.0 + 3.0 * jnp.arange(lag_total, dtype=F32) / lag_total
    station_ids = jnp.arange(stations, dtype=jnp.int32)

    def planes(rows):
        return [rows[:, i * bins : (i + 1) * bins].astype(F32) for i in range(comps * parts)]

    pairs_first = {ahead: [] for ahead in aheads}
    pairs_second = {behind: [] for behind in behinds}
    rounds = {}
    for ahead in aheads:
        for behind in behinds:
            if ahead + behind < steps:
                arrival = max(ahead, behind // reach, 1)
                later = arrival > 1 and ahead == arrival
                rounds.setdefault((arrival, later), []).append((ahead, behind))
    after = jnp.int32(0)
    arrived = 1
    for arrival, later in sorted(rounds):
        active = rounds[(arrival, later)]
        if arrival > arrived:
            arrived = arrival
            wait = after
        elif arrival == 1:
            wait = jnp.int32(0)
        picks = []
        rows = []
        crosses = []
        for ahead, behind in active:
            chosen = lists_of[ahead][ahead + behind] + wait
            pick_first = (chosen[:, 0:1] == station_ids[None, :]).astype(BF16)
            pick_second = (chosen[:, 1:2] == station_ids[None, :]).astype(BF16)
            a = planes(jnp.dot(pick_first, firsts[ahead], preferred_element_type=BF16))
            b = planes(jnp.dot(pick_second, seconds[behind], preferred_element_type=BF16))
            real = sum(a[2 * c] * b[2 * c] + a[2 * c + 1] * b[2 * c + 1] for c in range(comps))
            imag = sum(a[2 * c + 1] * b[2 * c] - a[2 * c] * b[2 * c + 1] for c in range(comps))
            picks.append((pick_first, pick_second))
            rows.append((a, b))
            crosses.append(jnp.concatenate([real, imag], 1).astype(BF16))
        cross = jnp.concatenate(crosses, 0)
        share = cross.shape[0] // lanes
        full = jnp.concatenate(
            swap_lanes([cross[j * share : (j + 1) * share] for j in range(lanes)], lane, lanes), 1
        )
        lagged = jnp.dot(full, table, preferred_element_type=F32)
        energy = jnp.sum(weight[None, :] * lagged * lagged, axis=1) / lag_total
        adjoint = (weight[None, :] * lagged / jnp.sqrt(energy + 1e-05)[:, None]).astype(BF16)
        spectral = lax.dot_general(
            adjoint, table, (((1,), (1,)), ((), ())), preferred_element_type=F32
        ).astype(BF16)
        after = jnp.minimum(jnp.abs(spectral[0, 0]), 0).astype(jnp.int32)
        mine = 2 * bins
        spectral = jnp.concatenate(
            swap_lanes([spectral[:, j * mine : (j + 1) * mine] for j in range(lanes)], lane, lanes), 0
        )
        for n, (ahead, behind) in enumerate(active):
            a, b = rows[n]
            listed = spectral[n * slots : (n + 1) * slots].astype(F32)
            real = listed[:, :bins]
            imag = listed[:, bins:]
            near = []
            far = []
            for c in range(comps):
                near += [real * b[2 * c] - imag * b[2 * c + 1], real * b[2 * c + 1] + imag * b[2 * c]]
                far += [real * a[2 * c] + imag * a[2 * c + 1], real * a[2 * c + 1] - imag * a[2 * c]]
            near = jnp.concatenate(near, 1).astype(BF16)
            far = jnp.concatenate(far, 1).astype(BF16)
            pairs_first[ahead].append((picks[n][0], near))
            pairs_second[behind].append((picks[n][1], far))

    def scatter(terms):
        picks = jnp.concatenate([pick for pick, _ in terms], 0)
        values = jnp.concatenate([value for _, value in terms], 0)
        return jnp.einsum("ps,pw->sw", picks, values, preferred_element_type=F32)

    from_ahead = jnp.zeros((), F32)
    from_back = jnp.zeros((), F32)
    for behind in behinds[:0:-1]:
        part = scatter(pairs_second[behind]) + from_back
        from_back = from_behind(part.astype(BF16), "blk", -reach).astype(F32)
    for ahead in aheads[:0:-1]:
        part = scatter(pairs_first[ahead]) + from_ahead
        from_ahead = from_behind(part.astype(BF16), "blk", 1).astype(F32)
    total = scatter(pairs_first[0] + pairs_second[0]) + from_back + from_ahead
    gradient = total / math.sqrt(slots)
    return gradient.reshape(stations, comps, parts, bins)


def solution(mesh):
    in_specs = (
        P("blk", None, None, "lag"),
        P("blk", None),
        P("blk", None, None, None),
        P("blk", None),
    )
    out_specs = P("blk", None, None, "lag")
    return jax.shard_map(
        on_device, mesh=mesh, in_specs=in_specs, out_specs=out_specs, check_vma=False
    )
```

```python
import math

import jax
import jax.numpy as jnp
import ml_dtypes
import numpy as np
from jax import lax
from jax.sharding import PartitionSpec as P

F32 = jnp.float32
BF16 = jnp.bfloat16


def from_behind(block, axis, distance):
    devices = range(lax.axis_size(axis))
    route = [((i - distance) % len(devices), i) for i in devices]
    return lax.ppermute(block, axis, route)


def phase_table(lanes, bins_local):
    freq_total = lanes * bins_local
    lag_total = 2 * freq_total
    turns = np.arange(freq_total)[:, None] * np.arange(lag_total)[None, :] % lag_total
    angle = turns.astype(np.float32) * np.float32(2.0 * np.pi / lag_total)
    factor = np.float32(1.0) / np.sqrt(np.float32(freq_total))
    table = np.stack([np.cos(angle) * factor, -np.sin(angle) * factor], 0)
    table = table.reshape(2, lanes, bins_local, lag_total).transpose(1, 0, 2, 3)
    return table.reshape(lanes * 2 * bins_local, lag_total).astype(ml_dtypes.bfloat16)


def whiten(spectra, band, freq_ids):
    values = spectra.astype(F32)
    meansq = jnp.mean(values * values, axis=(1, 2))
    inside = (freq_ids[None, :] >= band[:, 0:1]) & (freq_ids[None, :] < band[:, 1:2])
    factor = jnp.where(inside, 1.0 / jnp.sqrt(jnp.maximum(meansq, 0.25)), 0.0)
    return (values * factor[:, None, None, :]).astype(BF16)


def in_lane_order(own, received, lane, lanes):
    relative = [own] + received
    backward = [relative[(-m) % lanes] for m in range(lanes)]
    if lanes == 2:
        first = jnp.where(lane == 0, own, received[0])
        second = jnp.where(lane == 0, received[0], own)
        return [first, second]
    stacked = jnp.stack(backward + backward, 0)
    ordered = lax.dynamic_slice_in_dim(stacked, (lanes - lane) % lanes, lanes, 0)
    return [ordered[j] for j in range(lanes)]


def swap_lanes(pieces, lane, lanes):
    stacked = jnp.stack(pieces, 0)
    own = lax.dynamic_index_in_dim(stacked, lane, 0, keepdims=False)
    received = []
    for r in range(1, lanes):
        leaving = lax.dynamic_index_in_dim(stacked, (lane + r) % lanes, 0, keepdims=False)
        received.append(from_behind(leaving, "lag", r))
    return in_lane_order(own, received, lane, lanes)


def on_device(spectra, band, pair_lists, pair_counts):
    stations, comps, parts, bins = spectra.shape
    steps, slots = pair_lists.shape[1:3]
    lanes = lax.axis_size("lag")
    freq_total = bins * lanes
    lag_total = 2 * freq_total
    width = comps * parts * bins
    lane = lax.axis_index("lag")
    freq_ids = lane * bins + jnp.arange(bins, dtype=jnp.int32)
    reach = math.isqrt(steps - 1) + 1
    aheads = list(range(reach))
    behinds = list(range(0, steps, reach))

    slot_ids = jnp.arange(slots, dtype=jnp.int32)
    used = slot_ids[None, :] < pair_counts[0][:, None]
    lists = jnp.where(used[:, :, None], pair_lists[0], stations)
    lists_of = {0: lists}
    for ahead in aheads[1:]:
        lists_of[ahead] = from_behind(lists, "blk", -ahead)
    resident = whiten(spectra, band, freq_ids).reshape(stations, width)
    firsts = {0: resident}
    seconds = {0: resident}
    for behind in behinds[1:]:
        seconds[behind] = from_behind(seconds[behind - reach], "blk", reach)
    for ahead in aheads[1:]:
        firsts[ahead] = from_behind(firsts[ahead - 1], "blk", -1)

    table = jnp.asarray(phase_table(lanes, bins))
    weight = 1.0 + 3.0 * jnp.arange(lag_total, dtype=F32) / lag_total
    station_ids = jnp.arange(stations, dtype=jnp.int32)

    def planes(rows):
        return [rows[:, i * bins : (i + 1) * bins].astype(F32) for i in range(comps * parts)]

    pairs_first = {ahead: [] for ahead in aheads}
    pairs_second = {behind: [] for behind in behinds}
    rounds = {}
    for ahead in aheads:
        for behind in behinds:
            if ahead + behind < steps:
                arrival = max(ahead, behind // reach, 1)
                later = arrival > 1 and ahead == arrival
                rounds.setdefault((arrival, later), []).append((ahead, behind))
    after = jnp.int32(0)
    arrived = 1
    for arrival, later in sorted(rounds):
        active = rounds[(arrival, later)]
        if arrival > arrived:
            arrived = arrival
            wait = after
        elif arrival == 1:
            wait = jnp.int32(0)
        picks = []
        rows = []
        crosses = []
        for ahead, behind in active:
            chosen = lists_of[ahead][ahead + behind] + wait
            pick_first = (chosen[:, 0:1] == station_ids[None, :]).astype(BF16)
            pick_second = (chosen[:, 1:2] == station_ids[None, :]).astype(BF16)
            a = planes(jnp.dot(pick_first, firsts[ahead], preferred_element_type=BF16))
            b = planes(jnp.dot(pick_second, seconds[behind], preferred_element_type=BF16))
            real = sum(a[2 * c] * b[2 * c] + a[2 * c + 1] * b[2 * c + 1] for c in range(comps))
            imag = sum(a[2 * c + 1] * b[2 * c] - a[2 * c] * b[2 * c + 1] for c in range(comps))
            picks.append((pick_first, pick_second))
            rows.append((a, b))
            crosses.append(jnp.concatenate([real, imag], 1).astype(BF16))
        cross = jnp.concatenate(crosses, 0)
        share = cross.shape[0] // lanes
        full = jnp.concatenate(
            swap_lanes([cross[j * share : (j + 1) * share] for j in range(lanes)], lane, lanes), 1
        )
        lagged = jnp.dot(full, table, preferred_element_type=F32)
        energy = jnp.sum(weight[None, :] * lagged * lagged, axis=1) / lag_total
        adjoint = (weight[None, :] * lagged / jnp.sqrt(energy + 1e-05)[:, None]).astype(BF16)
        spectral = lax.dot_general(
            adjoint, table, (((1,), (1,)), ((), ())), preferred_element_type=F32
        ).astype(BF16)
        after = jnp.minimum(jnp.abs(spectral[0, 0]), 0).astype(jnp.int32)
        mine = 2 * bins
        spectral = jnp.concatenate(
            swap_lanes([spectral[:, j * mine : (j + 1) * mine] for j in range(lanes)], lane, lanes), 0
        )
        for n, (ahead, behind) in enumerate(active):
            a, b = rows[n]
            listed = spectral[n * slots : (n + 1) * slots].astype(F32)
            real = listed[:, :bins]
            imag = listed[:, bins:]
            near = []
            far = []
            for c in range(comps):
                near += [real * b[2 * c] - imag * b[2 * c + 1], real * b[2 * c + 1] + imag * b[2 * c]]
                far += [real * a[2 * c] + imag * a[2 * c + 1], real * a[2 * c + 1] - imag * a[2 * c]]
            near = jnp.concatenate(near, 1).astype(BF16)
            far = jnp.concatenate(far, 1).astype(BF16)
            pairs_first[ahead].append((picks[n][0], near))
            pairs_second[behind].append((picks[n][1], far))

    def scatter(terms):
        picks = jnp.concatenate([pick for pick, _ in terms], 0)
        values = jnp.concatenate([value for _, value in terms], 0)
        return jnp.einsum("ps,pw->sw", picks, values, preferred_element_type=F32)

    half = width // 2

    def send_back(terms, carried, distance):
        part = scatter(terms)
        halves = [part[:, :half], part[:, half:]]
        if carried is not None:
            halves = [x + y for x, y in zip(halves, carried)]
        return [from_behind(x.astype(BF16), "blk", distance).astype(F32) for x in halves]

    from_ahead = None
    from_back = None
    for behind in behinds[:0:-1]:
        from_back = send_back(pairs_second[behind], from_back, -reach)
    for ahead in aheads[:0:-1]:
        from_ahead = send_back(pairs_first[ahead], from_ahead, 1)
    total = scatter(pairs_first[0] + pairs_second[0])
    total = total + jnp.concatenate([x + y for x, y in zip(from_back, from_ahead)], 1)
    gradient = total / math.sqrt(slots)
    return gradient.reshape(stations, comps, parts, bins)


def solution(mesh):
    in_specs = (
        P("blk", None, None, "lag"),
        P("blk", None),
        P("blk", None, None, None),
        P("blk", None),
    )
    out_specs = P("blk", None, None, "lag")
    return jax.shard_map(
        on_device, mesh=mesh, in_specs=in_specs, out_specs=out_specs, check_vma=False
    )
```
